32 devices in a mesh: region: 4 (over z), sub: 8 (over y, x, core).
Axes of the slice: x: 2, y: 2, z: 4, core: 2. Of those that a mesh axis runs over, the one named last changes fastest.
Arguments:
- features: bfloat16 [96, 262144], P(None, ('region', 'sub')), may hold values from -60 to 60
- neighbors: int32 [27, 262144], P(None, ('region', 'sub')), may hold values from 0 to 12288, as said below
- send_rows: int32 [32, 4096], P(('region', 'sub')), may hold values from 0 to 8191, as said below
- active_rows: int32 [32], replicated, may hold values from 2048 to 8192, as said below
- weight_one: bfloat16 [27, 96, 96], replicated, may hold values from -0.125 to 0.125
- weight_two: bfloat16 [27, 96, 96], replicated, may hold values from -0.125 to 0.125
- norm_gain: float32 [2, 96], replicated, may hold values from 0.5 to 2
- norm_shift: float32 [2, 96], replicated, may hold values from -1 to 1
Outputs:
- refined: bfloat16 [96, 262144], P(None, ('region', 'sub'))
The draws below stay inside these ranges and needn't reach their ends.
Inputs may be any that keep to these rules, and one draw needn't show every extreme that they name: `active_rows`: each entry is a multiple of 128; the busiest device has all 8192 slots occupied; occupied slots come first. `send_rows`: row s lists in slots r * 128 to r * 128 + 127 the local columns of device s, below active_rows[s], whose features device r needs; any device r other than s may receive; the slots that carry voxels come first in each group of 128; a slot that carries nothing holds 0; in every draw some device receives all 128 slots from every other device. `neighbors`: an entry is a local column below the device's active count, an arrived column 8192 + p * 128 + c whose slot carries a voxel, or 12288 for a missing voxel; the middle offset of an active column names the column itself; inactive columns name no voxel; every slot that carries a voxel is named somewhere.
All inputs are finite; a program needn't handle non-finite values.
Results may differ from the reference program's by a relative error of at most 0.0052.
Values may be sent and summed in bfloat16 or wider, within the bound.
A program may use at most 128 MiB of HBM per device.

```python
import math
import jax
import jax.numpy as jnp
from jax import lax

C = 96
K3 = 27
BLOCK = 128
V_DEV = 8192
CAP = 128
DEVICES = 32


def active_counts(key):
    streams = jax.random.split(jax.random.fold_in(key, 7), 8)
    blocks = V_DEV // BLOCK
    lowest = max(1, blocks // 4)
    breadth = blocks - lowest
    draws_blk = jax.random.randint(streams[0], (DEVICES,), 0, breadth + 1)
    count_blk = lowest + draws_blk * draws_blk * draws_blk // max(breadth, 1) ** 2
    order = jax.random.permutation(streams[1], DEVICES)
    count_blk = count_blk.at[order[0]].set(blocks).at[order[1]].set(lowest)
    active = (count_blk * BLOCK).astype(jnp.int32)
    return (active, streams, order)


def layout(key):
    active, streams, order = active_counts(key)
    dev_ids = jnp.arange(DEVICES, dtype=jnp.int32)
    others = dev_ids[:, None] != dev_ids[None, :]
    sends = jax.random.randint(streams[2], (DEVICES, DEVICES), 0, CAP + 1)
    sends = jnp.where(others, sends, 0)
    sends = sends.at[:, order[2]].set(jnp.where(others[:, order[2]], CAP, 0))
    slot_ids = jnp.arange(CAP, dtype=jnp.int32)
    listed = jax.random.randint(streams[3], (DEVICES, DEVICES, CAP), 0, active[:, None, None])
    listed = jnp.where(slot_ids[None, None, :] < sends[:, :, None], listed, 0)
    send_table = listed.reshape(DEVICES, DEVICES * CAP).astype(jnp.int32)
    missing = V_DEV + DEVICES * CAP

    def device_map(dev_key, active_count, recv_counts):
        pieces = jax.random.split(dev_key, 4)
        columns = jnp.arange(V_DEV, dtype=jnp.int32)
        living = columns < active_count
        sort_kind = jax.random.randint(pieces[0], (K3, V_DEV), 0, 8)
        local_pick = jax.random.randint(pieces[1], (K3, V_DEV), 0, active_count)
        slots = jnp.arange(DEVICES * CAP, dtype=jnp.int32)
        carrying = slots % CAP < recv_counts[slots // CAP]
        slot_order = jnp.argsort(jnp.where(carrying, 0, 1) * (DEVICES * CAP) + slots, stable=True).astype(jnp.int32)
        held = jnp.sum(carrying.astype(jnp.int32))
        halo_pick = jax.random.randint(pieces[2], (K3, V_DEV), 0, jnp.maximum(held, 1))
        halo_ref = V_DEV + slot_order[halo_pick]
        kernel_map = jnp.where(sort_kind <= 1, missing, jnp.where(sort_kind == 7, jnp.where(held > 0, halo_ref, missing), local_pick))
        kernel_map = kernel_map.at[K3 // 2].set(columns)
        kernel_map = jnp.where(living[None, :], kernel_map, missing)
        flat_map = kernel_map.reshape(-1)
        usable = (living[None, :] & (jnp.arange(K3)[:, None] != K3 // 2)).reshape(-1)
        shuffle = jax.random.permutation(pieces[3], K3 * V_DEV)
        pos_order = jnp.argsort(jnp.where(usable, 0, 1) * (K3 * V_DEV) + shuffle, stable=True)
        targets = pos_order[:DEVICES * CAP]
        rank_ids = jnp.arange(DEVICES * CAP, dtype=jnp.int32)
        flat_map = flat_map.at[targets].set(jnp.where(rank_ids < held, V_DEV + slot_order, flat_map[targets]))
        return flat_map.reshape(K3, V_DEV).astype(jnp.int32)
    dev_keys = jax.random.split(streams[4], DEVICES)
    maps = jax.vmap(device_map)(dev_keys, active, sends.T)
    neighbor_table = jnp.transpose(maps, (1, 0, 2)).reshape(K3, DEVICES * V_DEV)
    return (active, send_table, neighbor_table)


def draw_active_rows(key, part):
    return layout(key)[0]


def draw_send_rows(key, part):
    return layout(key)[1]


def draw_neighbors(key, part):
    return layout(key)[2]


def draw_features(key, part):
    active = active_counts(key)[0]
    streams = jax.random.split(jax.random.fold_in(key, 11), 3)
    total_rows = DEVICES * V_DEV
    row_ids = jnp.arange(total_rows, dtype=jnp.int32)
    position = row_ids.astype(jnp.float32) / max(total_rows - 1, 1)
    owner = row_ids // V_DEV
    column = (row_ids % V_DEV).astype(jnp.float32)
    span = jnp.maximum(active[owner] - 1, 1).astype(jnp.float32)
    inner = jnp.clip(column / span, 0.0, 1.0)
    row_draw = jax.random.uniform(streams[0], (total_rows,), jnp.float32)
    col_draw = jax.random.uniform(streams[1], (C, 1), jnp.float32)
    row_scale = jnp.power(10.0, 0.35 * position + 0.45 * inner + 0.2 * row_draw)
    basis = jnp.clip(jax.random.normal(streams[2], (C, total_rows), jnp.float32), -6.0, 6.0)
    values = 0.1 * basis * row_scale[None, :] * jnp.power(10.0, col_draw)
    return values.astype(jnp.bfloat16)


def normal_values(own_key, dims, width, reach, kind=jnp.bfloat16):
    return jnp.clip(width * jax.random.normal(own_key, dims, jnp.float32), -reach, reach).astype(kind)


def setup_inputs(seed: int = 0) -> dict:
    key_of = jax.random.split(jax.random.key(seed), 9)
    features = draw_features(jax.random.fold_in(key_of[8], 71), 0)
    neighbors = draw_neighbors(jax.random.fold_in(key_of[8], 71), 0)
    send_rows = draw_send_rows(jax.random.fold_in(key_of[8], 71), 0)
    active_rows = draw_active_rows(jax.random.fold_in(key_of[8], 71), 0)
    weight_one = normal_values(key_of[4], (K3, C, C), (K3 * C) ** -0.5, 0.125)
    weight_two = normal_values(key_of[5], (K3, C, C), (K3 * C) ** -0.5, 0.125)
    norm_gain = jnp.clip(jnp.exp(jax.random.uniform(key_of[6], (2, C), jnp.float32, math.log(0.5), math.log(2.0))), 0.5, 2.0)
    norm_shift = jnp.clip(jax.random.uniform(key_of[7], (2, C), jnp.float32, -1.0, 1.0), -1.0, 1.0)
    return dict(features=features, neighbors=neighbors, send_rows=send_rows, active_rows=active_rows, weight_one=weight_one, weight_two=weight_two, norm_gain=norm_gain, norm_shift=norm_shift)


NORM_EPS = 1e-05

def gather_columns(extended, kernel_map, weight):
    gathered = jnp.take(extended, kernel_map, axis=1, mode='fill', fill_value=0)
    return jnp.einsum('ikb,kio->ob', gathered.astype(jnp.float32), weight.astype(jnp.float32))

def one_layer(hidden, neighbors, send_rows, active_rows, weight, gain, shift):

    def device_conv(device):
        own = lax.dynamic_slice_in_dim(hidden, device * V_DEV, V_DEV, 1)
        listed = lax.dynamic_slice_in_dim(send_rows, device * CAP, CAP, 1).astype(jnp.int32)
        sources = (jnp.arange(DEVICES, dtype=jnp.int32)[:, None] * V_DEV + listed).reshape(-1)
        arrived = jnp.take(hidden, sources, axis=1)
        extended = jnp.concatenate([own, arrived], axis=1)
        kernel_map = lax.dynamic_slice_in_dim(neighbors, device * V_DEV, V_DEV, 1)
        return gather_columns(extended, kernel_map, weight)
    conved = lax.map(device_conv, jnp.arange(DEVICES, dtype=jnp.int32))
    active = jnp.arange(V_DEV, dtype=jnp.int32)[None, None, :] < active_rows[:, None, None]
    population = jnp.sum(active_rows).astype(jnp.float32)
    average = lax.optimization_barrier(jnp.sum(jnp.where(active, conved, 0.0), axis=(0, 2))) / population
    offset = jnp.where(active, conved - average[None, :, None], 0.0)
    spread = lax.optimization_barrier(jnp.sum(offset * offset, axis=(0, 2))) / population
    factor = gain * lax.rsqrt(spread + NORM_EPS)
    normed = (conved - average[None, :, None]) * factor[None, :, None] + shift[None, :, None]
    normed = jnp.where(active, jnp.maximum(normed, 0.0), 0.0).astype(jnp.bfloat16)
    return jnp.transpose(normed, (1, 0, 2)).reshape(normed.shape[1], -1)

def reference(features, neighbors, send_rows, active_rows, weight_one, weight_two, norm_gain, norm_shift):
    level_one = one_layer(features, neighbors, send_rows, active_rows, weight_one, norm_gain[0], norm_shift[0])
    return one_layer(level_one, neighbors, send_rows, active_rows, weight_two, norm_gain[1], norm_shift[1])
```

```python
import functools

import jax
import jax.numpy as jnp
from jax import lax
from jax.experimental import pallas as pl
from jax.experimental.pallas import tpu as pltpu
from jax.sharding import PartitionSpec as P

NORM_EPS = 1e-05
LANES = 128
PAD = 8
STEP = 512
GROUP = 16
AXES = ("region", "sub")


def conv_kernel(
    live_ref, index_ref, local_ref, arrived_ref, weight_ref, out_ref, stat_ref, table, staged
):
    step = pl.program_id(0)
    live = live_ref[0]
    rows = local_ref.shape[0]
    halo = arrived_ref.shape[0]
    offsets = index_ref.shape[0]
    middle = offsets // 2

    @pl.when(step == 0)
    def fill():
        zeros = jnp.zeros((PAD, LANES), jnp.float32)
        table[pl.ds(0, PAD), :] = zeros
        table[pl.ds(PAD + rows + halo, PAD), :] = zeros

        def move(source, base):
            def one(turn, carry):
                start = pl.multiple_of(turn * 128, 128)
                table[pl.ds(start + base, 128), :] = source[pl.ds(start, 128), :].astype(
                    jnp.float32
                )
                return carry

            lax.fori_loop(0, source.shape[0] // 128, one, 0)

        move(local_ref, PAD)
        move(arrived_ref, PAD + rows)

    first = step * STEP

    @pl.when(first < live)
    def work():
        sublane = lax.broadcasted_iota(jnp.int32, (8, LANES), 0)

        def collect(turn, carry):
            start = pl.multiple_of(turn * GROUP, GROUP)
            for k in range(offsets):
                if k == middle:
                    block = local_ref[pl.ds(pl.multiple_of(first + start, GROUP), GROUP), :]
                else:
                    halves = []
                    for half in range(GROUP // 8):
                        held = None
                        for s in range(8):
                            place = index_ref[k, start + half * 8 + s] + (PAD - s)
                            window = table[pl.ds(place, 8), :]
                            held = window if s == 0 else jnp.where(sublane == s, window, held)
                        halves.append(held)
                    block = jnp.concatenate(halves, axis=0).astype(jnp.bfloat16)
                staged[pl.ds(start, GROUP), pl.ds(k * LANES, LANES)] = block
            return carry

        lax.fori_loop(0, STEP // GROUP, collect, 0)
        out_ref[pl.ds(pl.multiple_of(first, STEP), STEP), :] = jnp.dot(
            staged[...], weight_ref[...], preferred_element_type=jnp.float32
        )

    @pl.when(step == pl.num_programs(0) - 1)
    def finish():
        blocks = live // LANES

        def total(turn, carry):
            start = pl.multiple_of(turn * LANES, LANES)
            return carry + jnp.sum(out_ref[pl.ds(start, LANES), :], axis=0, keepdims=True)

        summed = lax.fori_loop(0, blocks, total, jnp.zeros((1, LANES), jnp.float32))
        mean = summed / live.astype(jnp.float32)

        def spread(turn, carry):
            start = pl.multiple_of(turn * LANES, LANES)
            offset = out_ref[pl.ds(start, LANES), :] - mean
            return carry + jnp.sum(offset * offset, axis=0, keepdims=True)

        squared = lax.fori_loop(0, blocks, spread, jnp.zeros((1, LANES), jnp.float32))
        row = lax.broadcasted_iota(jnp.int32, (8, LANES), 0)
        stat_ref[...] = jnp.where(row == 0, mean, jnp.where(row == 1, squared, 0.0))


def convolve(live, neighbors, local, arrived, weight):
    offsets, rows = neighbors.shape
    halo = arrived.shape[0]
    whole = lambda shape: pl.BlockSpec(shape, lambda i: (0,) * len(shape))
    return pl.pallas_call(
        conv_kernel,
        grid=(rows // STEP,),
        in_specs=[
            pl.BlockSpec(memory_space=pltpu.SMEM),
            pl.BlockSpec((offsets, STEP), lambda i: (0, i), memory_space=pltpu.SMEM),
            whole((rows, LANES)),
            whole((halo, LANES)),
            whole((offsets * LANES, LANES)),
        ],
        out_specs=[whole((rows, LANES)), whole((8, LANES))],
        out_shape=[
            jax.ShapeDtypeStruct((rows, LANES), jnp.float32),
            jax.ShapeDtypeStruct((8, LANES), jnp.float32),
        ],
        scratch_shapes=[
            pltpu.VMEM((PAD + rows + halo + PAD, LANES), jnp.float32),
            pltpu.VMEM((STEP, offsets * LANES), jnp.bfloat16),
        ],
        compiler_params=pltpu.CompilerParams(vmem_limit_bytes=52 * 1024 * 1024),
        cost_estimate=pl.CostEstimate(
            flops=2 * rows * offsets * LANES * LANES,
            bytes_accessed=rows * LANES * 10,
            transcendentals=0,
        ),
        name="conv",
    )(live, neighbors, local, arrived, weight)


def route(local, outgoing):
    parcel = jnp.take(local, outgoing, axis=0, mode="clip")
    return lax.all_to_all(parcel, AXES, split_axis=0, concat_axis=0, tiled=True)


def widen(weight):
    offsets, fan_in, fan_out = weight.shape
    padded = jnp.pad(weight, ((0, 0), (0, LANES - fan_in), (0, LANES - fan_out)))
    return padded.reshape(offsets * LANES, LANES)


def body(
    features, neighbors, send_rows, active_rows, weight_one, weight_two, norm_gain, norm_shift
):
    device = lax.axis_index(AXES)
    channels, extent = features.shape
    live = lax.dynamic_slice_in_dim(active_rows, device, 1)
    active = (jnp.arange(extent, dtype=jnp.int32) < live[0])[:, None]
    counts = active_rows.astype(jnp.float32)[:, None]
    population = jnp.sum(active_rows).astype(jnp.float32)
    outgoing = send_rows[0]
    local = jnp.pad(jnp.transpose(features), ((0, 0), (0, LANES - channels)))
    fill = ((0, 0), (0, LANES - channels))
    gains = jnp.pad(norm_gain, fill)
    shifts = jnp.pad(norm_shift, fill)
    for depth, weight in enumerate((weight_one, weight_two)):
        arrived = route(local, outgoing)
        conved, stats = convolve(live, neighbors, local, arrived, widen(weight))
        every = lax.all_gather(stats[:2], AXES, axis=0, tiled=False)
        average = jnp.sum(every[:, 0] * counts, axis=0) / population
        apart = every[:, 0] - average
        spread = jnp.sum(every[:, 1] + counts * apart * apart, axis=0) / population
        factor = gains[depth] * lax.rsqrt(spread + NORM_EPS)
        normed = (conved - average) * factor + shifts[depth]
        local = jnp.where(active, jnp.maximum(normed, 0.0), 0.0).astype(jnp.bfloat16)
    return jnp.transpose(local[:, :channels])


def solution(mesh):
    placed = (
        P(None, AXES),
        P(None, AXES),
        P(AXES, None),
        P(),
        P(),
        P(),
        P(),
        P(),
    )
    return jax.shard_map(
        body, mesh=mesh, in_specs=placed, out_specs=P(None, AXES), check_vma=False
    )
```

```python
import functools

import jax
import jax.numpy as jnp
from jax import lax
from jax.experimental import pallas as pl
from jax.experimental.pallas import tpu as pltpu
from jax.sharding import PartitionSpec as P

NORM_EPS = 1e-05
LANES = 128
PAD = 8
BLOCK = 128
LEAST = 2048
STEP = 512
GROUP = 16
AXES = ("region", "sub")
MESH = pl.DeviceIdType.MESH


def conv_kernel(
    job_ref, index_ref, local_ref, arrived_ref, weight_ref, out_ref, stat_ref, table, staged
):
    step = pl.program_id(0)
    live = job_ref[0]
    base = job_ref[1]
    rows = local_ref.shape[0]
    halo = arrived_ref.shape[0]
    offsets = index_ref.shape[0]
    middle = offsets // 2

    @pl.when((step == 0) & (live > 0))
    def fill():
        zeros = jnp.zeros((PAD, LANES), jnp.float32)
        table[pl.ds(0, PAD), :] = zeros
        table[pl.ds(PAD + rows + halo, PAD), :] = zeros

        def move(source, base):
            def one(turn, carry):
                start = pl.multiple_of(turn * 128, 128)
                table[pl.ds(start + base, 128), :] = source[pl.ds(start, 128), :].astype(
                    jnp.float32
                )
                return carry

            lax.fori_loop(0, source.shape[0] // 128, one, 0)

        move(local_ref, PAD)
        move(arrived_ref, PAD + rows)

    first = step * STEP

    @pl.when(first < live)
    def work():
        sublane = lax.broadcasted_iota(jnp.int32, (8, LANES), 0)

        def collect(turn, carry):
            start = pl.multiple_of(turn * GROUP, GROUP)
            for k in range(offsets):
                if k == middle:
                    own = pl.multiple_of(base + first + start, GROUP)
                    block = local_ref[pl.ds(own, GROUP), :]
                else:
                    halves = []
                    for half in range(GROUP // 8):
                        held = None
                        for s in range(8):
                            place = index_ref[k, start + (half * 8 + s)]
                            window = table[pl.ds(place, 8), :]
                            held = window if s == 0 else jnp.where(sublane == s, window, held)
                        halves.append(held)
                    block = jnp.concatenate(halves, axis=0).astype(jnp.bfloat16)
                staged[pl.ds(start, GROUP), pl.ds(k * LANES, LANES)] = block
            return carry

        lax.fori_loop(0, jnp.minimum(STEP, live - first) // GROUP, collect, 0)
        out_ref[pl.ds(pl.multiple_of(first, STEP), STEP), :] = jnp.dot(
            staged[...], weight_ref[...], preferred_element_type=jnp.float32
        )

    @pl.when(step == pl.num_programs(0) - 1)
    def finish():
        blocks = live // LANES

        def total(turn, carry):
            start = pl.multiple_of(turn * LANES, LANES)
            return carry + jnp.sum(out_ref[pl.ds(start, LANES), :], axis=0, keepdims=True)

        summed = lax.fori_loop(0, blocks, total, jnp.zeros((1, LANES), jnp.float32))
        mean = summed / jnp.maximum(live, 1).astype(jnp.float32)

        def spread(turn, carry):
            start = pl.multiple_of(turn * LANES, LANES)
            offset = out_ref[pl.ds(start, LANES), :] - mean
            return carry + jnp.sum(offset * offset, axis=0, keepdims=True)

        squared = lax.fori_loop(0, blocks, spread, jnp.zeros((1, LANES), jnp.float32))
        row = lax.broadcasted_iota(jnp.int32, (8, LANES), 0)
        stat_ref[...] = jnp.where(row == 0, mean, jnp.where(row == 1, squared, 0.0))


def convolve(job, indices, local, arrived, weight, room):
    offsets, rows = indices.shape
    extent = local.shape[0]
    halo = arrived.shape[0]
    whole = lambda shape: pl.BlockSpec(shape, lambda i, job: (0,) * len(shape))

    def columns(i, job):
        return (0, jnp.minimum(i, jnp.maximum(job[0] - 1, 0) // STEP))

    return pl.pallas_call(
        conv_kernel,
        grid_spec=pltpu.PrefetchScalarGridSpec(
            num_scalar_prefetch=1,
            grid=(rows // STEP,),
            in_specs=[
                pl.BlockSpec((offsets, STEP), columns, memory_space=pltpu.SMEM),
                whole((extent, LANES)),
                whole((halo, LANES)),
                whole((offsets * LANES, LANES)),
            ],
            out_specs=[whole((rows + room, LANES)), whole((8, LANES))],
            scratch_shapes=[
                pltpu.VMEM((PAD + extent + halo + PAD, LANES), jnp.float32),
                pltpu.VMEM((STEP, offsets * LANES), jnp.bfloat16),
            ],
        ),
        out_shape=[
            jax.ShapeDtypeStruct((rows + room, LANES), jnp.float32),
            jax.ShapeDtypeStruct((8, LANES), jnp.float32),
        ],
        compiler_params=pltpu.CompilerParams(vmem_limit_bytes=56 * 1024 * 1024),
        cost_estimate=pl.CostEstimate(
            flops=20 * rows * offsets * LANES * LANES,
            bytes_accessed=rows * LANES * 100,
            transcendentals=0,
        ),
        name="conv",
    )(job, indices, local, arrived, weight)


def share_kernel(regions, subs, mine_ref, every_ref, send_sem, recv_sem):
    devices = regions * subs
    me = lax.axis_index("region") * subs + lax.axis_index("sub")
    place = lambda p: (lax.div(p, subs), lax.rem(p, subs))
    barrier = pltpu.get_barrier_semaphore()

    def greet(off, carry):
        other = lax.rem(me + off, devices)
        pl.semaphore_signal(barrier, inc=1, device_id=place(other), device_id_type=MESH)
        return carry

    lax.fori_loop(1, devices, greet, 0)
    pl.semaphore_wait(barrier, devices - 1)

    def copy(off, slot):
        return pltpu.make_async_remote_copy(
            src_ref=mine_ref,
            dst_ref=every_ref.at[slot],
            send_sem=send_sem.at[off],
            recv_sem=recv_sem.at[off],
            device_id=place(lax.rem(me + off, devices)),
            device_id_type=MESH,
        )

    def send(off, carry):
        copy(off, me).start()
        return carry

    def finish(off, carry):
        copy(off, me).wait_send()
        copy(off, lax.rem(me + devices - off, devices)).wait_recv()
        return carry

    lax.fori_loop(1, devices, send, 0)
    every_ref[me] = mine_ref[...]
    lax.fori_loop(1, devices, finish, 0)


def share(mine, regions, subs):
    devices = regions * subs
    return pl.pallas_call(
        functools.partial(share_kernel, regions, subs),
        out_shape=jax.ShapeDtypeStruct((devices,) + mine.shape, mine.dtype),
        in_specs=[pl.BlockSpec(memory_space=pltpu.VMEM)],
        out_specs=pl.BlockSpec(memory_space=pltpu.VMEM),
        scratch_shapes=[
            pltpu.SemaphoreType.DMA((devices,)),
            pltpu.SemaphoreType.DMA((devices,)),
        ],
        compiler_params=pltpu.CompilerParams(collective_id=0, has_side_effects=True),
        name="share",
    )(mine)


def route(local, outgoing):
    parcel = jnp.take(local, outgoing, axis=0, mode="clip")
    return lax.all_to_all(parcel, AXES, split_axis=0, concat_axis=0, tiled=True)


def widen(weight):
    offsets, fan_in, fan_out = weight.shape
    padded = jnp.pad(weight, ((0, 0), (0, LANES - fan_in), (0, LANES - fan_out)))
    return padded.reshape(offsets * LANES, LANES)


def body(
    regions,
    subs,
    features,
    neighbors,
    send_rows,
    active_rows,
    weight_one,
    weight_two,
    norm_gain,
    norm_shift,
):
    device = lax.axis_index(AXES)
    channels, extent = features.shape
    reach = (extent - LEAST) // 2
    pairs = [(s, s ^ 1) for s in range(subs)]
    swap = lambda value: lax.ppermute(value, "sub", pairs)
    live = active_rows[device]
    active = (jnp.arange(extent, dtype=jnp.int32) < live)[:, None]
    population = jnp.sum(active_rows).astype(jnp.float32)
    twin_rows = active_rows.reshape(-1, 2)[:, ::-1].reshape(-1)
    given_rows = jnp.maximum(active_rows - twin_rows, 0) // (2 * BLOCK) * BLOCK
    taken_rows = given_rows.reshape(-1, 2)[:, ::-1].reshape(-1)
    kept_rows = active_rows - given_rows
    kept = kept_rows[device]
    taken = taken_rows[device]
    counts = jnp.stack([kept_rows, taken_rows], axis=1).astype(jnp.float32)[:, :, None]
    outgoing = send_rows[0]
    local = jnp.pad(jnp.transpose(features), ((0, 0), (0, LANES - channels)))
    indices = neighbors + (PAD - jnp.arange(extent, dtype=jnp.int32) % 8)[None, :]
    handed = lax.dynamic_slice_in_dim(jnp.pad(indices, ((0, 0), (0, reach))), kept, reach, 1)
    borrowed = swap(handed)
    own_job = jnp.stack([kept, jnp.zeros_like(kept)])
    twin_job = jnp.stack([taken, kept_rows[device ^ 1]])
    fill = ((0, 0), (0, LANES - channels))
    gains = jnp.pad(norm_gain, fill)
    shifts = jnp.pad(norm_shift, fill)
    for depth, weight in enumerate((weight_one, weight_two)):
        wide = widen(weight)
        arrived = route(local, outgoing)
        twin_local = swap(local)
        twin_arrived = swap(arrived)
        conved, own_stats = convolve(own_job, indices, local, arrived, wide, reach)
        helped, twin_stats = convolve(twin_job, borrowed, twin_local, twin_arrived, wide, 0)
        returned = swap(helped)
        mine = jnp.concatenate([own_stats[:2], twin_stats[:2], jnp.zeros_like(own_stats[:4])])
        every = share(mine, regions, subs)
        means, squares = every[:, 0:4:2], every[:, 1:4:2]
        average = jnp.sum(means * counts, axis=(0, 1)) / population
        apart = means - average
        spread = jnp.sum(squares + counts * apart * apart, axis=(0, 1)) / population
        factor = gains[depth] * lax.rsqrt(spread + NORM_EPS)
        conved = lax.dynamic_update_slice_in_dim(conved, returned, kept, 0)[:extent]
        normed = (conved - average) * factor + shifts[depth]
        local = jnp.where(active, jnp.maximum(normed, 0.0), 0.0).astype(jnp.bfloat16)
    return jnp.transpose(local[:, :channels])


def solution(mesh):
    placed = (
        P(None, AXES),
        P(None, AXES),
        P(AXES, None),
        P(),
        P(),
        P(),
        P(),
        P(),
    )
    return jax.shard_map(
        functools.partial(body, mesh.shape["region"], mesh.shape["sub"]),
        mesh=mesh,
        in_specs=placed,
        out_specs=P(None, AXES),
        check_vma=False,
    )
```

```python
import functools

import jax
import jax.numpy as jnp
from jax import lax
from jax.experimental import pallas as pl
from jax.experimental.pallas import tpu as pltpu
from jax.sharding import PartitionSpec as P

NORM_EPS = 1e-05
LANES = 128
PAD = 8
BLOCK = 128
LEAST = 2048
STEP = 512
GROUP = 16
AXES = ("region", "sub")
MESH = pl.DeviceIdType.MESH


def conv_kernel(
    job_ref, index_ref, local_ref, arrived_ref, weight_ref, out_ref, stat_ref, table, staged
):
    step = pl.program_id(0)
    live = job_ref[0]
    base = job_ref[1]
    rows = local_ref.shape[0]
    halo = arrived_ref.shape[0]
    offsets = index_ref.shape[1]
    middle = offsets // 2

    @pl.when((step == 0) & (live > 0))
    def fill():
        zeros = jnp.zeros((PAD, LANES), jnp.float32)
        table[pl.ds(0, PAD), :] = zeros
        table[pl.ds(PAD + rows + halo, PAD), :] = zeros

        def move(source, base):
            def one(turn, carry):
                start = pl.multiple_of(turn * 128, 128)
                table[pl.ds(start + base, 128), :] = source[pl.ds(start, 128), :].astype(
                    jnp.float32
                )
                return carry

            lax.fori_loop(0, source.shape[0] // 128, one, 0)

        move(local_ref, PAD)
        move(arrived_ref, PAD + rows)

    first = step * STEP

    @pl.when(first < live)
    def work():
        sublane = lax.broadcasted_iota(jnp.int32, (8, LANES), 0)

        def gather(index_row, k, start):
            for group in range(BLOCK // GROUP):
                halves = []
                for half in range(GROUP // 8):
                    held = None
                    for s in range(8):
                        place = index_ref[index_row, k, group * GROUP + half * 8 + s]
                        window = table[pl.ds(place, 8), :]
                        held = window if s == 0 else jnp.where(sublane == s, window, held)
                    halves.append(held)
                staged[k, pl.ds(pl.multiple_of(start + group * GROUP, GROUP), GROUP), :] = (
                    jnp.concatenate(halves, axis=0).astype(jnp.bfloat16)
                )

        def collect(block, carry):
            start = pl.multiple_of(block * BLOCK, BLOCK)
            own = pl.multiple_of(base + first + start, BLOCK)
            staged[middle, pl.ds(start, BLOCK), :] = local_ref[pl.ds(own, BLOCK), :]

            def pair(turn, carry):
                gather(block, turn, start)
                gather(block, turn + (middle + 1), start)
                return carry

            lax.fori_loop(0, middle, pair, 0)
            return carry

        lax.fori_loop(0, jnp.minimum(STEP, live - first) // BLOCK, collect, 0)
        wide = jnp.concatenate([staged[k] for k in range(offsets)], axis=1)
        out_ref[pl.ds(pl.multiple_of(first, STEP), STEP), :] = jnp.dot(
            wide, weight_ref[...], preferred_element_type=jnp.float32
        )

    @pl.when(step == pl.num_programs(0) - 1)
    def finish():
        blocks = live // LANES

        def total(turn, carry):
            start = pl.multiple_of(turn * LANES, LANES)
            return carry + jnp.sum(out_ref[pl.ds(start, LANES), :], axis=0, keepdims=True)

        summed = lax.fori_loop(0, blocks, total, jnp.zeros((1, LANES), jnp.float32))
        mean = summed / jnp.maximum(live, 1).astype(jnp.float32)

        def spread(turn, carry):
            start = pl.multiple_of(turn * LANES, LANES)
            offset = out_ref[pl.ds(start, LANES), :] - mean
            return carry + jnp.sum(offset * offset, axis=0, keepdims=True)

        squared = lax.fori_loop(0, blocks, spread, jnp.zeros((1, LANES), jnp.float32))
        row = lax.broadcasted_iota(jnp.int32, (8, LANES), 0)
        stat_ref[...] = jnp.where(row == 0, mean, jnp.where(row == 1, squared, 0.0))


def convolve(job, indices, local, arrived, weight, room):
    blocks, offsets, _ = indices.shape
    rows = blocks * BLOCK
    extent = local.shape[0]
    halo = arrived.shape[0]
    whole = lambda shape: pl.BlockSpec(shape, lambda i, job: (0,) * len(shape))

    def columns(i, job):
        return (jnp.minimum(i, jnp.maximum(job[0] - 1, 0) // STEP), 0, 0)

    return pl.pallas_call(
        conv_kernel,
        grid_spec=pltpu.PrefetchScalarGridSpec(
            num_scalar_prefetch=1,
            grid=(rows // STEP,),
            in_specs=[
                pl.BlockSpec(
                    (STEP // BLOCK, offsets, BLOCK), columns, memory_space=pltpu.SMEM
                ),
                whole((extent, LANES)),
                whole((halo, LANES)),
                whole((offsets * LANES, LANES)),
            ],
            out_specs=[whole((rows + room, LANES)), whole((8, LANES))],
            scratch_shapes=[
                pltpu.VMEM((PAD + extent + halo + PAD, LANES), jnp.float32),
                pltpu.VMEM((offsets, STEP, LANES), jnp.bfloat16),
            ],
        ),
        out_shape=[
            jax.ShapeDtypeStruct((rows + room, LANES), jnp.float32),
            jax.ShapeDtypeStruct((8, LANES), jnp.float32),
        ],
        compiler_params=pltpu.CompilerParams(vmem_limit_bytes=56 * 1024 * 1024),
        cost_estimate=pl.CostEstimate(
            flops=20 * rows * offsets * LANES * LANES,
            bytes_accessed=rows * LANES * 100,
            transcendentals=0,
        ),
        name="conv",
    )(job, indices, local, arrived, weight)


def share_kernel(regions, subs, mine_ref, every_ref, send_sem, recv_sem):
    devices = regions * subs
    me = lax.axis_index("region") * subs + lax.axis_index("sub")
    place = lambda p: (lax.div(p, subs), lax.rem(p, subs))
    barrier = pltpu.get_barrier_semaphore()

    def greet(off, carry):
        other = lax.rem(me + off, devices)
        pl.semaphore_signal(barrier, inc=1, device_id=place(other), device_id_type=MESH)
        return carry

    lax.fori_loop(1, devices, greet, 0)
    pl.semaphore_wait(barrier, devices - 1)

    def copy(off, slot):
        return pltpu.make_async_remote_copy(
            src_ref=mine_ref,
            dst_ref=every_ref.at[slot],
            send_sem=send_sem.at[off],
            recv_sem=recv_sem.at[off],
            device_id=place(lax.rem(me + off, devices)),
            device_id_type=MESH,
        )

    def send(off, carry):
        copy(off, me).start()
        return carry

    def finish(off, carry):
        copy(off, me).wait_send()
        copy(off, lax.rem(me + devices - off, devices)).wait_recv()
        return carry

    lax.fori_loop(1, devices, send, 0)
    every_ref[me] = mine_ref[...]
    lax.fori_loop(1, devices, finish, 0)


def share(mine, regions, subs):
    devices = regions * subs
    return pl.pallas_call(
        functools.partial(share_kernel, regions, subs),
        out_shape=jax.ShapeDtypeStruct((devices,) + mine.shape, mine.dtype),
        in_specs=[pl.BlockSpec(memory_space=pltpu.VMEM)],
        out_specs=pl.BlockSpec(memory_space=pltpu.VMEM),
        scratch_shapes=[
            pltpu.SemaphoreType.DMA((devices,)),
            pltpu.SemaphoreType.DMA((devices,)),
        ],
        compiler_params=pltpu.CompilerParams(collective_id=0, has_side_effects=True),
        name="share",
    )(mine)


def route(local, outgoing):
    parcel = jnp.take(local, outgoing, axis=0, mode="clip")
    return lax.all_to_all(parcel, AXES, split_axis=0, concat_axis=0, tiled=True)


def widen(weight):
    offsets, fan_in, fan_out = weight.shape
    padded = jnp.pad(weight, ((0, 0), (0, LANES - fan_in), (0, LANES - fan_out)))
    return padded.reshape(offsets * LANES, LANES)


def body(
    regions,
    subs,
    features,
    neighbors,
    send_rows,
    active_rows,
    weight_one,
    weight_two,
    norm_gain,
    norm_shift,
):
    device = lax.axis_index(AXES)
    channels, extent = features.shape
    reach = (extent - LEAST) // 2
    pairs = [(s, s ^ 1) for s in range(subs)]
    swap = lambda value: lax.ppermute(value, "sub", pairs)
    live = active_rows[device]
    active = (jnp.arange(extent, dtype=jnp.int32) < live)[:, None]
    population = jnp.sum(active_rows).astype(jnp.float32)
    twin_rows = active_rows.reshape(-1, 2)[:, ::-1].reshape(-1)
    given_rows = jnp.maximum(active_rows - twin_rows, 0) // (2 * BLOCK) * BLOCK
    taken_rows = given_rows.reshape(-1, 2)[:, ::-1].reshape(-1)
    kept_rows = active_rows - given_rows
    kept = kept_rows[device]
    taken = taken_rows[device]
    counts = jnp.stack([kept_rows, taken_rows], axis=1).astype(jnp.float32)[:, :, None]
    outgoing = send_rows[0]
    local = jnp.pad(jnp.transpose(features), ((0, 0), (0, LANES - channels)))
    indices = neighbors + (PAD - jnp.arange(extent, dtype=jnp.int32) % 8)[None, :]
    indices = jnp.transpose(indices.reshape(indices.shape[0], -1, BLOCK), (1, 0, 2))
    padded = jnp.pad(indices, ((0, reach // BLOCK), (0, 0), (0, 0)))
    handed = lax.dynamic_slice_in_dim(padded, kept // BLOCK, reach // BLOCK, 0)
    borrowed = swap(handed)
    own_job = jnp.stack([kept, jnp.zeros_like(kept)])
    twin_job = jnp.stack([taken, kept_rows[device ^ 1]])
    fill = ((0, 0), (0, LANES - channels))
    gains = jnp.pad(norm_gain, fill)
    shifts = jnp.pad(norm_shift, fill)
    for depth, weight in enumerate((weight_one, weight_two)):
        wide = widen(weight)
        arrived = route(local, outgoing)
        twin_local = swap(local)
        twin_arrived = swap(arrived)
        conved, own_stats = convolve(own_job, indices, local, arrived, wide, reach)
        later_job, own_stats = lax.optimization_barrier((twin_job, own_stats))
        helped, twin_stats = convolve(later_job, borrowed, twin_local, twin_arrived, wide, 0)
        returned = swap(helped)
        mine = jnp.concatenate([own_stats[:2], twin_stats[:2], jnp.zeros_like(own_stats[:4])])
        every = share(mine, regions, subs)
        means, squares = every[:, 0:4:2], every[:, 1:4:2]
        average = jnp.sum(means * counts, axis=(0, 1)) / population
        apart = means - average
        spread = jnp.sum(squares + counts * apart * apart, axis=(0, 1)) / population
        factor = gains[depth] * lax.rsqrt(spread + NORM_EPS)
        conved = lax.dynamic_update_slice_in_dim(conved, returned, kept, 0)[:extent]
        normed = (conved - average) * factor + shifts[depth]
        local = jnp.where(active, jnp.maximum(normed, 0.0), 0.0).astype(jnp.bfloat16)
    return jnp.transpose(local[:, :channels])


def solution(mesh):
    placed = (
        P(None, AXES),
        P(None, AXES),
        P(AXES, None),
        P(),
        P(),
        P(),
        P(),
        P(),
    )
    return jax.shard_map(
        functools.partial(body, mesh.shape["region"], mesh.shape["sub"]),
        mesh=mesh,
        in_specs=placed,
        out_specs=P(None, AXES),
        check_vma=False,
    )
```

```python
import functools

import jax
import jax.numpy as jnp
from jax import lax
from jax.experimental import pallas as pl
from jax.experimental.pallas import tpu as pltpu
from jax.sharding import PartitionSpec as P

NORM_EPS = 1e-05
LANES = 128
PAD = 8
BLOCK = 128
LEAST = 2048
STEP = 512
GROUP = 16
AXES = ("region", "sub")
MESH = pl.DeviceIdType.MESH


def pick(table, index_of, store):
    sublane = lax.broadcasted_iota(jnp.int32, (8, LANES), 0)
    for group in range(BLOCK // GROUP):
        halves = []
        for half in range(GROUP // 8):
            held = None
            for s in range(8):
                window = table[pl.ds(index_of(group * GROUP + half * 8 + s), 8), :]
                held = window if s == 0 else jnp.where(sublane == s, window, held)
            halves.append(held)
        store(group * GROUP, jnp.concatenate(halves, axis=0).astype(jnp.bfloat16))


def conv_kernel(
    job_ref, index_ref, local_ref, arrived_ref, weight_ref, out_ref, stat_ref, table, staged
):
    step = pl.program_id(0)
    live = job_ref[0]
    base = job_ref[1]
    rows = local_ref.shape[0]
    halo = arrived_ref.shape[0]
    offsets = index_ref.shape[1]
    middle = offsets // 2

    @pl.when((step == 0) & (live > 0))
    def fill():
        zeros = jnp.zeros((PAD, LANES), jnp.float32)
        table[pl.ds(0, PAD), :] = zeros
        table[pl.ds(PAD + rows + halo, PAD), :] = zeros

        def move(source, base):
            def one(turn, carry):
                start = pl.multiple_of(turn * 128, 128)
                table[pl.ds(start + base, 128), :] = source[pl.ds(start, 128), :].astype(
                    jnp.float32
                )
                return carry

            lax.fori_loop(0, source.shape[0] // 128, one, 0)

        move(local_ref, PAD)
        move(arrived_ref, PAD + rows)

    first = step * STEP

    @pl.when(first < live)
    def work():
        def store(k, row, value):
            staged[k, pl.ds(pl.multiple_of(row, GROUP), GROUP), :] = value

        def collect(block, carry):
            start = pl.multiple_of(block * BLOCK, BLOCK)
            own = pl.multiple_of(base + first + start, BLOCK)
            staged[middle, pl.ds(start, BLOCK), :] = local_ref[pl.ds(own, BLOCK), :]

            def pair(turn, carry):
                for k in (turn, turn + (middle + 1)):
                    pick(
                        table,
                        lambda c, k=k: index_ref[block, k, c],
                        lambda c, value, k=k: store(k, start + c, value),
                    )
                return carry

            lax.fori_loop(0, middle, pair, 0)
            return carry

        lax.fori_loop(0, jnp.minimum(STEP, live - first) // BLOCK, collect, 0)
        wide = jnp.concatenate([staged[k] for k in range(offsets)], axis=1)
        out_ref[pl.ds(pl.multiple_of(first, STEP), STEP), :] = jnp.dot(
            wide, weight_ref[...], preferred_element_type=jnp.float32
        )

    @pl.when(step == pl.num_programs(0) - 1)
    def finish():
        blocks = live // LANES

        def total(turn, carry):
            start = pl.multiple_of(turn * LANES, LANES)
            return carry + jnp.sum(out_ref[pl.ds(start, LANES), :], axis=0, keepdims=True)

        summed = lax.fori_loop(0, blocks, total, jnp.zeros((1, LANES), jnp.float32))
        mean = summed / jnp.maximum(live, 1).astype(jnp.float32)

        def spread(turn, carry):
            start = pl.multiple_of(turn * LANES, LANES)
            offset = out_ref[pl.ds(start, LANES), :] - mean
            return carry + jnp.sum(offset * offset, axis=0, keepdims=True)

        squared = lax.fori_loop(0, blocks, spread, jnp.zeros((1, LANES), jnp.float32))
        row = lax.broadcasted_iota(jnp.int32, (8, LANES), 0)
        stat_ref[...] = jnp.where(row == 0, mean, jnp.where(row == 1, squared, 0.0))


def convolve(job, indices, local, arrived, weight):
    blocks, offsets, _ = indices.shape
    rows = blocks * BLOCK
    extent = local.shape[0]
    halo = arrived.shape[0]
    whole = lambda shape: pl.BlockSpec(shape, lambda i, job: (0,) * len(shape))

    def columns(i, job):
        return (jnp.minimum(i, jnp.maximum(job[0] - 1, 0) // STEP), 0, 0)

    return pl.pallas_call(
        conv_kernel,
        grid_spec=pltpu.PrefetchScalarGridSpec(
            num_scalar_prefetch=1,
            grid=(rows // STEP,),
            in_specs=[
                pl.BlockSpec(
                    (STEP // BLOCK, offsets, BLOCK), columns, memory_space=pltpu.SMEM
                ),
                whole((extent, LANES)),
                whole((halo, LANES)),
                whole((offsets * LANES, LANES)),
            ],
            out_specs=[whole((rows, LANES)), whole((8, LANES))],
            scratch_shapes=[
                pltpu.VMEM((PAD + extent + halo + PAD, LANES), jnp.float32),
                pltpu.VMEM((offsets, STEP, LANES), jnp.bfloat16),
            ],
        ),
        out_shape=[
            jax.ShapeDtypeStruct((rows, LANES), jnp.float32),
            jax.ShapeDtypeStruct((8, LANES), jnp.float32),
        ],
        compiler_params=pltpu.CompilerParams(vmem_limit_bytes=56 * 1024 * 1024),
        cost_estimate=pl.CostEstimate(
            flops=20 * rows * offsets * LANES * LANES,
            bytes_accessed=rows * LANES * 100,
            transcendentals=0,
        ),
        name="conv",
    )(job, indices, local, arrived, weight)


def share_kernel(regions, subs, mine_ref, every_ref, send_sem, recv_sem):
    devices = regions * subs
    me = lax.axis_index("region") * subs + lax.axis_index("sub")
    place = lambda p: (lax.div(p, subs), lax.rem(p, subs))
    barrier = pltpu.get_barrier_semaphore()

    def greet(off, carry):
        other = lax.rem(me + off, devices)
        pl.semaphore_signal(barrier, inc=1, device_id=place(other), device_id_type=MESH)
        return carry

    lax.fori_loop(1, devices, greet, 0)
    pl.semaphore_wait(barrier, devices - 1)

    def copy(off, slot):
        return pltpu.make_async_remote_copy(
            src_ref=mine_ref,
            dst_ref=every_ref.at[slot],
            send_sem=send_sem.at[off],
            recv_sem=recv_sem.at[off],
            device_id=place(lax.rem(me + off, devices)),
            device_id_type=MESH,
        )

    def send(off, carry):
        copy(off, me).start()
        return carry

    def finish(off, carry):
        copy(off, me).wait_send()
        copy(off, lax.rem(me + devices - off, devices)).wait_recv()
        return carry

    lax.fori_loop(1, devices, send, 0)
    every_ref[me] = mine_ref[...]
    lax.fori_loop(1, devices, finish, 0)


def share(mine, regions, subs):
    devices = regions * subs
    return pl.pallas_call(
        functools.partial(share_kernel, regions, subs),
        out_shape=jax.ShapeDtypeStruct((devices,) + mine.shape, mine.dtype),
        in_specs=[pl.BlockSpec(memory_space=pltpu.VMEM)],
        out_specs=pl.BlockSpec(memory_space=pltpu.VMEM),
        scratch_shapes=[
            pltpu.SemaphoreType.DMA((devices,)),
            pltpu.SemaphoreType.DMA((devices,)),
        ],
        compiler_params=pltpu.CompilerParams(collective_id=0, has_side_effects=True),
        name="share",
    )(mine)


def parcel_rows(table, send_ref, parcel_ref):
    def one(turn, carry):
        start = pl.multiple_of(turn * BLOCK, BLOCK)

        def store(c, value):
            parcel_ref[pl.ds(pl.multiple_of(start + c, GROUP), GROUP), :] = value

        pick(table, lambda c: send_ref[turn, c], store)
        return carry

    lax.fori_loop(0, send_ref.shape[0], one, 0)


def clear_edges(table):
    zeros = jnp.zeros((PAD, LANES), jnp.float32)
    table[pl.ds(0, PAD), :] = zeros
    table[pl.ds(table.shape[0] - PAD, PAD), :] = zeros


def open_kernel(send_ref, features_ref, local_ref, parcel_ref, table):
    clear_edges(table)
    channels, extent = features_ref.shape

    def one(turn, carry):
        start = pl.multiple_of(turn * BLOCK, BLOCK)
        block = features_ref[:, pl.ds(start, BLOCK)].astype(jnp.float32)
        rest = jnp.zeros((LANES - channels, BLOCK), jnp.float32)
        turned = jnp.concatenate([block, rest], axis=0).T
        table[pl.ds(start + PAD, BLOCK), :] = turned
        local_ref[pl.ds(start, BLOCK), :] = turned.astype(jnp.bfloat16)
        return carry

    lax.fori_loop(0, extent // BLOCK, one, 0)
    parcel_rows(table, send_ref, parcel_ref)


def normalizer(counts_ref, every_ref, gain_ref, shift_ref):
    devices = every_ref.shape[0]
    zero = jnp.zeros((1, LANES), jnp.float32)

    def add(p, carry):
        total, population = carry
        first, second = counts_ref[0, p], counts_ref[1, p]
        total = total + every_ref[p, 0:1, :] * first + every_ref[p, 2:3, :] * second
        return total, population + first + second

    total, population = lax.fori_loop(0, devices, add, (zero, jnp.float32(0)))
    average = total / population

    def widen_by(p, total):
        first, second = counts_ref[0, p], counts_ref[1, p]
        near = every_ref[p, 0:1, :] - average
        far = every_ref[p, 2:3, :] - average
        return (
            total
            + (every_ref[p, 1:2, :] + near * near * first)
            + (every_ref[p, 3:4, :] + far * far * second)
        )

    spread = lax.fori_loop(0, devices, widen_by, zero) / population
    factor = gain_ref[...] * lax.rsqrt(spread + NORM_EPS)
    shift = shift_ref[...]
    return lambda rows: jnp.maximum((rows - average) * factor + shift, 0.0)


def settle(job_ref, conved_ref, returned_ref, normal, put):
    live, kept = job_ref[0], job_ref[1]

    def near(turn, carry):
        start = pl.multiple_of(turn * BLOCK, BLOCK)
        put(start, normal(conved_ref[pl.ds(start, BLOCK), :]))
        return carry

    def far(turn, carry):
        start = pl.multiple_of(turn * BLOCK, BLOCK)
        source = pl.multiple_of(start - kept, BLOCK)
        put(start, normal(returned_ref[pl.ds(source, BLOCK), :]))
        return carry

    def idle(turn, carry):
        put(pl.multiple_of(turn * BLOCK, BLOCK), jnp.zeros((BLOCK, LANES), jnp.float32))
        return carry

    lax.fori_loop(0, kept // BLOCK, near, 0)
    lax.fori_loop(kept // BLOCK, live // BLOCK, far, 0)
    lax.fori_loop(live // BLOCK, conved_ref.shape[0] // BLOCK, idle, 0)


def middle_kernel(
    job_ref,
    counts_ref,
    send_ref,
    every_ref,
    gain_ref,
    shift_ref,
    conved_ref,
    returned_ref,
    local_ref,
    parcel_ref,
    table,
):
    clear_edges(table)
    normal = normalizer(counts_ref, every_ref, gain_ref, shift_ref)

    def put(start, rows):
        table[pl.ds(start + PAD, BLOCK), :] = rows
        local_ref[pl.ds(start, BLOCK), :] = rows.astype(jnp.bfloat16)

    settle(job_ref, conved_ref, returned_ref, normal, put)
    parcel_rows(table, send_ref, parcel_ref)


def close_kernel(
    job_ref, counts_ref, every_ref, gain_ref, shift_ref, conved_ref, returned_ref, out_ref
):
    normal = normalizer(counts_ref, every_ref, gain_ref, shift_ref)
    channels = out_ref.shape[0]

    def put(start, rows):
        out_ref[:, pl.ds(start, BLOCK)] = rows.T[:channels].astype(jnp.bfloat16)

    settle(job_ref, conved_ref, returned_ref, normal, put)


def local_call(kernel, scalars, values, outs, scratch, name):
    smem = pl.BlockSpec(memory_space=pltpu.SMEM)
    vmem = pl.BlockSpec(memory_space=pltpu.VMEM)
    shapes = [jax.ShapeDtypeStruct(shape, jnp.bfloat16) for shape in outs]
    return pl.pallas_call(
        kernel,
        in_specs=[smem] * len(scalars) + [vmem] * len(values),
        out_specs=[vmem] * len(outs),
        out_shape=shapes,
        scratch_shapes=scratch,
        compiler_params=pltpu.CompilerParams(vmem_limit_bytes=40 * 1024 * 1024),
        name=name,
    )(*scalars, *values)


def route(parcel):
    return lax.all_to_all(parcel, AXES, split_axis=0, concat_axis=0, tiled=True)


def widen(weight):
    offsets, fan_in, fan_out = weight.shape
    padded = jnp.pad(weight, ((0, 0), (0, LANES - fan_in), (0, LANES - fan_out)))
    return padded.reshape(offsets * LANES, LANES)


def body(
    regions,
    subs,
    features,
    neighbors,
    send_rows,
    active_rows,
    weight_one,
    weight_two,
    norm_gain,
    norm_shift,
):
    device = lax.axis_index(AXES)
    channels, extent = features.shape
    reach = (extent - LEAST) // 2
    pairs = [(s, s ^ 1) for s in range(subs)]
    swap = lambda value: lax.ppermute(value, "sub", pairs)
    live = active_rows[device]
    twin_rows = active_rows.reshape(-1, 2)[:, ::-1].reshape(-1)
    given_rows = jnp.maximum(active_rows - twin_rows, 0) // (2 * BLOCK) * BLOCK
    taken_rows = given_rows.reshape(-1, 2)[:, ::-1].reshape(-1)
    kept_rows = active_rows - given_rows
    kept = kept_rows[device]
    taken = taken_rows[device]
    counts = jnp.stack([kept_rows, taken_rows]).astype(jnp.float32)
    nudge = PAD - jnp.arange(extent, dtype=jnp.int32) % 8
    outgoing = send_rows[0].reshape(-1, BLOCK) + nudge[:BLOCK]
    table = [pltpu.VMEM((PAD + extent + PAD, LANES), jnp.float32)]
    rows_out = [(extent, LANES), (send_rows.shape[1], LANES)]
    local, parcel = local_call(open_kernel, [outgoing], [features], rows_out, table, "open")
    indices = neighbors + nudge[None, :]
    indices = jnp.transpose(indices.reshape(indices.shape[0], -1, BLOCK), (1, 0, 2))
    padded = jnp.pad(indices, ((0, reach // BLOCK), (0, 0), (0, 0)))
    handed = lax.dynamic_slice_in_dim(padded, kept // BLOCK, reach // BLOCK, 0)
    borrowed = swap(handed)
    own_job = jnp.stack([kept, jnp.zeros_like(kept)])
    twin_job = jnp.stack([taken, kept_rows[device ^ 1]])
    fill = ((0, 0), (0, LANES - channels))
    gains = jnp.pad(norm_gain, fill)
    shifts = jnp.pad(norm_shift, fill)
    for depth, weight in enumerate((weight_one, weight_two)):
        wide = widen(weight)
        arrived = route(parcel)
        twin_local = swap(local)
        twin_arrived = swap(arrived)
        conved, own_stats = convolve(own_job, indices, local, arrived, wide)
        later_job, own_stats = lax.optimization_barrier((twin_job, own_stats))
        helped, twin_stats = convolve(later_job, borrowed, twin_local, twin_arrived, wide)
        returned = swap(helped)
        mine = jnp.concatenate([own_stats[:2], twin_stats[:2], jnp.zeros_like(own_stats[:4])])
        every = share(mine, regions, subs)
        merge_job = jnp.stack([live, kept])
        gain, shift = gains[depth][None], shifts[depth][None]
        values = [every, gain, shift, conved, returned]
        if depth == 0:
            local, parcel = local_call(
                middle_kernel, [merge_job, counts, outgoing], values, rows_out, table, "middle"
            )
    (refined,) = local_call(
        close_kernel, [merge_job, counts], values, [(channels, extent)], [], "close"
    )
    return refined


def solution(mesh):
    placed = (
        P(None, AXES),
        P(None, AXES),
        P(AXES, None),
        P(),
        P(),
        P(),
        P(),
        P(),
    )
    return jax.shard_map(
        functools.partial(body, mesh.shape["region"], mesh.shape["sub"]),
        mesh=mesh,
        in_specs=placed,
        out_specs=P(None, AXES),
        check_vma=False,
    )
```

```python
import functools

import jax
import jax.numpy as jnp
from jax import lax
from jax.experimental import pallas as pl
from jax.experimental.pallas import tpu as pltpu
from jax.sharding import PartitionSpec as P

NORM_EPS = 1e-05
LANES = 128
PAD = 8
BLOCK = 128
LEAST = 2048
STEP = 512
GROUP = 16
RUN = 3
AXES = ("region", "sub")
MESH = pl.DeviceIdType.MESH


def pick(table, index_of, store):
    sublane = lax.broadcasted_iota(jnp.int32, (8, LANES), 0)
    for group in range(BLOCK // GROUP):
        halves = []
        for half in range(GROUP // 8):
            held = None
            for s in range(8):
                window = table[pl.ds(index_of(group * GROUP + half * 8 + s), 8), :]
                held = window if s == 0 else jnp.where(sublane == s, window, held)
            halves.append(held)
        store(group * GROUP, jnp.concatenate(halves, axis=0).astype(jnp.bfloat16))


def conv_kernel(
    job_ref, index_ref, local_ref, arrived_ref, weight_ref, out_ref, stat_ref, table, staged
):
    step = pl.program_id(0)
    live = job_ref[0]
    base = job_ref[1]
    rows = local_ref.shape[0]
    halo = arrived_ref.shape[0]
    offsets = index_ref.shape[1]
    middle = offsets // 2

    @pl.when((step == 0) & (live > 0))
    def fill():
        zeros = jnp.zeros((PAD, LANES), jnp.float32)
        table[pl.ds(0, PAD), :] = zeros
        table[pl.ds(PAD + rows + halo, PAD), :] = zeros

        def move(source, base):
            def one(turn, carry):
                start = pl.multiple_of(turn * 128, 128)
                table[pl.ds(start + base, 128), :] = source[pl.ds(start, 128), :].astype(
                    jnp.float32
                )
                return carry

            lax.fori_loop(0, source.shape[0] // 128, one, 0)

        move(local_ref, PAD)
        move(arrived_ref, PAD + rows)

    first = step * STEP

    @pl.when(first < live)
    def work():
        def store(k, row, value):
            staged[k, pl.ds(pl.multiple_of(row, GROUP), GROUP), :] = value

        def collect(block, carry):
            start = pl.multiple_of(block * BLOCK, BLOCK)
            own = pl.multiple_of(base + first + start, BLOCK)
            staged[middle, pl.ds(start, BLOCK), :] = local_ref[pl.ds(own, BLOCK), :]

            def pair(turn):
                for k in (turn, turn + (middle + 1)):
                    pick(
                        table,
                        lambda c, k=k: index_ref[block, k, c],
                        lambda c, value, k=k: store(k, start + c, value),
                    )

            def several(turn, carry):
                for part in range(RUN):
                    pair(turn * RUN + part)
                return carry

            lax.fori_loop(0, middle // RUN, several, 0)
            for turn in range(middle // RUN * RUN, middle):
                pair(turn)
            return carry

        lax.fori_loop(0, jnp.minimum(STEP, live - first) // BLOCK, collect, 0)
        wide = jnp.concatenate([staged[k] for k in range(offsets)], axis=1)
        out_ref[pl.ds(pl.multiple_of(first, STEP), STEP), :] = jnp.dot(
            wide, weight_ref[...], preferred_element_type=jnp.float32
        )

    @pl.when(step == pl.num_programs(0) - 1)
    def finish():
        blocks = live // LANES

        def total(turn, carry):
            start = pl.multiple_of(turn * LANES, LANES)
            return carry + jnp.sum(out_ref[pl.ds(start, LANES), :], axis=0, keepdims=True)

        summed = lax.fori_loop(0, blocks, total, jnp.zeros((1, LANES), jnp.float32))
        mean = summed / jnp.maximum(live, 1).astype(jnp.float32)

        def spread(turn, carry):
            start = pl.multiple_of(turn * LANES, LANES)
            offset = out_ref[pl.ds(start, LANES), :] - mean
            return carry + jnp.sum(offset * offset, axis=0, keepdims=True)

        squared = lax.fori_loop(0, blocks, spread, jnp.zeros((1, LANES), jnp.float32))
        row = lax.broadcasted_iota(jnp.int32, (8, LANES), 0)
        stat_ref[...] = jnp.where(row == 0, mean, jnp.where(row == 1, squared, 0.0))


def convolve(job, indices, local, arrived, weight):
    blocks, offsets, _ = indices.shape
    rows = blocks * BLOCK
    extent = local.shape[0]
    halo = arrived.shape[0]
    whole = lambda shape: pl.BlockSpec(shape, lambda i, job: (0,) * len(shape))

    def columns(i, job):
        return (jnp.minimum(i, jnp.maximum(job[0] - 1, 0) // STEP), 0, 0)

    return pl.pallas_call(
        conv_kernel,
        grid_spec=pltpu.PrefetchScalarGridSpec(
            num_scalar_prefetch=1,
            grid=(rows // STEP,),
            in_specs=[
                pl.BlockSpec(
                    (STEP // BLOCK, offsets, BLOCK), columns, memory_space=pltpu.SMEM
                ),
                whole((extent, LANES)),
                whole((halo, LANES)),
                whole((offsets * LANES, LANES)),
            ],
            out_specs=[whole((rows, LANES)), whole((8, LANES))],
            scratch_shapes=[
                pltpu.VMEM((PAD + extent + halo + PAD, LANES), jnp.float32),
                pltpu.VMEM((offsets, STEP, LANES), jnp.bfloat16),
            ],
        ),
        out_shape=[
            jax.ShapeDtypeStruct((rows, LANES), jnp.float32),
            jax.ShapeDtypeStruct((8, LANES), jnp.float32),
        ],
        compiler_params=pltpu.CompilerParams(vmem_limit_bytes=56 * 1024 * 1024),
        cost_estimate=pl.CostEstimate(
            flops=20 * rows * offsets * LANES * LANES,
            bytes_accessed=rows * LANES * 100,
            transcendentals=0,
        ),
        name="conv",
    )(job, indices, local, arrived, weight)


def share_kernel(
    regions, subs, own_ref, twin_ref, every_ref, mine_ref, send_sem, recv_sem
):
    devices = regions * subs
    me = lax.axis_index("region") * subs + lax.axis_index("sub")
    place = lambda p: (lax.div(p, subs), lax.rem(p, subs))
    mine_ref[pl.ds(0, 2), :] = own_ref[pl.ds(0, 2), :]
    mine_ref[pl.ds(2, 2), :] = twin_ref[pl.ds(0, 2), :]
    mine_ref[pl.ds(4, 4), :] = jnp.zeros((4, LANES), jnp.float32)
    barrier = pltpu.get_barrier_semaphore()

    def greet(off, carry):
        other = lax.rem(me + off, devices)
        pl.semaphore_signal(barrier, inc=1, device_id=place(other), device_id_type=MESH)
        return carry

    lax.fori_loop(1, devices, greet, 0)
    pl.semaphore_wait(barrier, devices - 1)

    def copy(off, slot):
        return pltpu.make_async_remote_copy(
            src_ref=mine_ref,
            dst_ref=every_ref.at[slot],
            send_sem=send_sem.at[off],
            recv_sem=recv_sem.at[off],
            device_id=place(lax.rem(me + off, devices)),
            device_id_type=MESH,
        )

    def send(off, carry):
        copy(off, me).start()
        return carry

    def finish(off, carry):
        copy(off, me).wait_send()
        copy(off, lax.rem(me + devices - off, devices)).wait_recv()
        return carry

    lax.fori_loop(1, devices, send, 0)
    every_ref[me] = mine_ref[...]
    lax.fori_loop(1, devices, finish, 0)


def share(own, twin, regions, subs):
    devices = regions * subs
    return pl.pallas_call(
        functools.partial(share_kernel, regions, subs),
        out_shape=jax.ShapeDtypeStruct((devices,) + own.shape, own.dtype),
        in_specs=[pl.BlockSpec(memory_space=pltpu.VMEM)] * 2,
        out_specs=pl.BlockSpec(memory_space=pltpu.VMEM),
        scratch_shapes=[
            pltpu.VMEM(own.shape, own.dtype),
            pltpu.SemaphoreType.DMA((devices,)),
            pltpu.SemaphoreType.DMA((devices,)),
        ],
        compiler_params=pltpu.CompilerParams(collective_id=0, has_side_effects=True),
        name="share",
    )(own, twin)


def parcel_rows(table, send_ref, parcel_ref):
    def one(turn, carry):
        start = pl.multiple_of(turn * BLOCK, BLOCK)

        def store(c, value):
            parcel_ref[pl.ds(pl.multiple_of(start + c, GROUP), GROUP), :] = value

        pick(table, lambda c: send_ref[turn, c], store)
        return carry

    lax.fori_loop(0, send_ref.shape[0], one, 0)


def clear_edges(table):
    zeros = jnp.zeros((PAD, LANES), jnp.float32)
    table[pl.ds(0, PAD), :] = zeros
    table[pl.ds(table.shape[0] - PAD, PAD), :] = zeros


def open_kernel(send_ref, features_ref, local_ref, parcel_ref, table):
    clear_edges(table)
    channels, extent = features_ref.shape

    def one(turn, carry):
        start = pl.multiple_of(turn * BLOCK, BLOCK)
        block = features_ref[:, pl.ds(start, BLOCK)].astype(jnp.float32)
        rest = jnp.zeros((LANES - channels, BLOCK), jnp.float32)
        turned = jnp.concatenate([block, rest], axis=0).T
        table[pl.ds(start + PAD, BLOCK), :] = turned
        local_ref[pl.ds(start, BLOCK), :] = turned.astype(jnp.bfloat16)
        return carry

    lax.fori_loop(0, extent // BLOCK, one, 0)
    parcel_rows(table, send_ref, parcel_ref)


def normalizer(counts_ref, every_ref, gain_ref, shift_ref):
    devices = every_ref.shape[0]
    zero = jnp.zeros((1, LANES), jnp.float32)

    def add(p, carry):
        total, population = carry
        first, second = counts_ref[0, p], counts_ref[1, p]
        total = total + every_ref[p, 0:1, :] * first + every_ref[p, 2:3, :] * second
        return total, population + first + second

    total, population = lax.fori_loop(0, devices, add, (zero, jnp.float32(0)))
    average = total / population

    def widen_by(p, total):
        first, second = counts_ref[0, p], counts_ref[1, p]
        near = every_ref[p, 0:1, :] - average
        far = every_ref[p, 2:3, :] - average
        return (
            total
            + (every_ref[p, 1:2, :] + near * near * first)
            + (every_ref[p, 3:4, :] + far * far * second)
        )

    spread = lax.fori_loop(0, devices, widen_by, zero) / population
    factor = gain_ref[...] * lax.rsqrt(spread + NORM_EPS)
    shift = shift_ref[...]
    return lambda rows: jnp.maximum((rows - average) * factor + shift, 0.0)


def settle(job_ref, conved_ref, returned_ref, normal, put):
    live, kept = job_ref[0], job_ref[1]

    def near(turn, carry):
        start = pl.multiple_of(turn * BLOCK, BLOCK)
        put(start, normal(conved_ref[pl.ds(start, BLOCK), :]))
        return carry

    def far(turn, carry):
        start = pl.multiple_of(turn * BLOCK, BLOCK)
        source = pl.multiple_of(start - kept, BLOCK)
        put(start, normal(returned_ref[pl.ds(source, BLOCK), :]))
        return carry

    def idle(turn, carry):
        put(pl.multiple_of(turn * BLOCK, BLOCK), jnp.zeros((BLOCK, LANES), jnp.float32))
        return carry

    lax.fori_loop(0, kept // BLOCK, near, 0)
    lax.fori_loop(kept // BLOCK, live // BLOCK, far, 0)
    lax.fori_loop(live // BLOCK, conved_ref.shape[0] // BLOCK, idle, 0)


def middle_kernel(
    job_ref,
    counts_ref,
    send_ref,
    every_ref,
    gain_ref,
    shift_ref,
    conved_ref,
    returned_ref,
    local_ref,
    parcel_ref,
    table,
):
    clear_edges(table)
    normal = normalizer(counts_ref, every_ref, gain_ref, shift_ref)

    def put(start, rows):
        table[pl.ds(start + PAD, BLOCK), :] = rows
        local_ref[pl.ds(start, BLOCK), :] = rows.astype(jnp.bfloat16)

    settle(job_ref, conved_ref, returned_ref, normal, put)
    parcel_rows(table, send_ref, parcel_ref)


def close_kernel(
    job_ref, counts_ref, every_ref, gain_ref, shift_ref, conved_ref, returned_ref, out_ref
):
    normal = normalizer(counts_ref, every_ref, gain_ref, shift_ref)
    channels = out_ref.shape[0]

    def put(start, rows):
        out_ref[:, pl.ds(start, BLOCK)] = rows.T[:channels].astype(jnp.bfloat16)

    settle(job_ref, conved_ref, returned_ref, normal, put)


def local_call(kernel, scalars, values, outs, scratch, name):
    smem = pl.BlockSpec(memory_space=pltpu.SMEM)
    vmem = pl.BlockSpec(memory_space=pltpu.VMEM)
    shapes = [jax.ShapeDtypeStruct(shape, jnp.bfloat16) for shape in outs]
    return pl.pallas_call(
        kernel,
        in_specs=[smem] * len(scalars) + [vmem] * len(values),
        out_specs=[vmem] * len(outs),
        out_shape=shapes,
        scratch_shapes=scratch,
        compiler_params=pltpu.CompilerParams(vmem_limit_bytes=40 * 1024 * 1024),
        name=name,
    )(*scalars, *values)


def route(parcel):
    return lax.all_to_all(parcel, AXES, split_axis=0, concat_axis=0, tiled=True)


def widen(weight):
    offsets, fan_in, fan_out = weight.shape
    padded = jnp.pad(weight, ((0, 0), (0, LANES - fan_in), (0, LANES - fan_out)))
    return padded.reshape(offsets * LANES, LANES)


def body(
    regions,
    subs,
    features,
    neighbors,
    send_rows,
    active_rows,
    weight_one,
    weight_two,
    norm_gain,
    norm_shift,
):
    device = lax.axis_index(AXES)
    channels, extent = features.shape
    reach = (extent - LEAST) // 2
    pairs = [(s, s ^ 1) for s in range(subs)]
    swap = lambda value: lax.ppermute(value, "sub", pairs)
    live = active_rows[device]
    twin_rows = active_rows.reshape(-1, 2)[:, ::-1].reshape(-1)
    given_rows = jnp.maximum(active_rows - twin_rows, 0) // (2 * BLOCK) * BLOCK
    taken_rows = given_rows.reshape(-1, 2)[:, ::-1].reshape(-1)
    kept_rows = active_rows - given_rows
    kept = kept_rows[device]
    taken = taken_rows[device]
    counts = jnp.stack([kept_rows, taken_rows]).astype(jnp.float32)
    nudge = PAD - jnp.arange(extent, dtype=jnp.int32) % 8
    outgoing = send_rows[0].reshape(-1, BLOCK) + nudge[:BLOCK]
    table = [pltpu.VMEM((PAD + extent + PAD, LANES), jnp.float32)]
    rows_out = [(extent, LANES), (send_rows.shape[1], LANES)]
    local, parcel = local_call(open_kernel, [outgoing], [features], rows_out, table, "open")
    indices = neighbors + nudge[None, :]
    indices = jnp.transpose(indices.reshape(indices.shape[0], -1, BLOCK), (1, 0, 2))
    padded = jnp.pad(indices, ((0, reach // BLOCK), (0, 0), (0, 0)))
    handed = lax.dynamic_slice_in_dim(padded, kept // BLOCK, reach // BLOCK, 0)
    borrowed = swap(handed)
    own_job = jnp.stack([kept, jnp.zeros_like(kept)])
    twin_job = jnp.stack([taken, kept_rows[device ^ 1]])
    fill = ((0, 0), (0, LANES - channels))
    gains = jnp.pad(norm_gain, fill)
    shifts = jnp.pad(norm_shift, fill)
    for depth, weight in enumerate((weight_one, weight_two)):
        wide = widen(weight)
        arrived = route(parcel)
        twin_local = swap(local)
        twin_arrived = swap(arrived)
        conved, own_stats = convolve(own_job, indices, local, arrived, wide)
        later_job, own_stats = lax.optimization_barrier((twin_job, own_stats))
        helped, twin_stats = convolve(later_job, borrowed, twin_local, twin_arrived, wide)
        returned = swap(helped)
        every = share(own_stats, twin_stats, regions, subs)
        merge_job = jnp.stack([live, kept])
        gain, shift = gains[depth][None], shifts[depth][None]
        values = [every, gain, shift, conved, returned]
        if depth == 0:
            local, parcel = local_call(
                middle_kernel, [merge_job, counts, outgoing], values, rows_out, table, "middle"
            )
    (refined,) = local_call(
        close_kernel, [merge_job, counts], values, [(channels, extent)], [], "close"
    )
    return refined


def solution(mesh):
    placed = (
        P(None, AXES),
        P(None, AXES),
        P(AXES, None),
        P(),
        P(),
        P(),
        P(),
        P(),
    )
    return jax.shard_map(
        functools.partial(body, mesh.shape["region"], mesh.shape["sub"]),
        mesh=mesh,
        in_specs=placed,
        out_specs=P(None, AXES),
        check_vma=False,
    )
```
